256 devices in a mesh: section: 4 (over z_lo, core), seq: 64 (over y, x, z_hi).
Axes of the slice: x: 4, y: 4, z: 8 (z_hi: 4, z_lo: 2; z = z_hi * 2 + z_lo), core: 2. Of those that a mesh axis runs over, the one named last changes fastest.
Arguments:
- acts_in: bfloat16 [4, 8192, 4096], P('section', 'seq'), may hold values from -8 to 8
- first_in: bfloat16 [8192, 4096], P('seq'), may hold values from -8 to 8
- saved_one: bfloat16 [4, 8192, 4096], P('section', 'seq'), may hold values from -8 to 8
- cot_one: bfloat16 [4, 8192, 4096], P('section', 'seq'), may hold values from -6 to 6
- saved_two: bfloat16 [4, 8192, 4096], P('section', 'seq'), may hold values from -8 to 8
- cot_last: bfloat16 [8192, 4096], P('seq'), may hold values from -6 to 6
- gains: float32 [4, 3, 4096], P('section'), may hold values from 0.1 to 1.9
- slopes: float32 [4, 32], P('section'), may hold values from 0.003 to 0.5
- ocean: int32 [8192], replicated, may hold values from 0 to 1, as said below
- places: int32 [2, 8192], replicated, may hold values from 0 to 63
Outputs:
- out_one: bfloat16 [4, 8192, 4096], P('section', 'seq')
- grad_one: bfloat16 [4, 8192, 4096], P('section', 'seq')
- fwd_two: bfloat16 [4, 8192, 4096], P('section', 'seq')
- bwd_two: bfloat16 [4, 8192, 4096], P('section', 'seq')
- gain_grads: float32 [4, 3, 4096], P('section')
The draws below stay inside these ranges and needn't reach their ends.
Inputs may be any that keep to these rules, and one draw needn't show every extreme that they name: The first patch of every region of 256 patches is ocean.
All inputs are finite; a program needn't handle non-finite values.
Results may differ from the reference program's by a relative error of at most 0.034.
Values may be sent and summed in bfloat16 or wider, within the bound.
No kernel may reach another device: no remote copies, remote signals or barrier semaphores. Data moves between devices by JAX's collectives and lax.ppermute only.
A program may use at most 192 MiB of HBM per device.

```python
import math
import jax
import jax.numpy as jnp
from jax import lax

D = 4096
HEADS = 32
HD = 128
REGION = 256
TOK_DEV = 128
SECTIONS = 4
TOKENS = 8192


def drawn_draw(key, shape):
    return jax.random.truncated_normal(key, -6.0, 6.0, shape, jnp.float32).astype(jnp.bfloat16)


def draw_acts_in(key, part):
    key = jax.random.fold_in(key, 1)
    return drawn_draw(key, (SECTIONS, TOKENS, D))


def draw_first_in(key, part):
    key = jax.random.fold_in(key, 2)
    return drawn_draw(key, (TOKENS, D))


def draw_saved_one(key, part):
    key = jax.random.fold_in(key, 3)
    return drawn_draw(key, (SECTIONS, TOKENS, D))


def draw_saved_two(key, part):
    key = jax.random.fold_in(key, 4)
    return drawn_draw(key, (SECTIONS, TOKENS, D))


def draw_ocean(key, part):
    key = jax.random.fold_in(key, 7)
    key_limit, key_roll = jax.random.split(key)
    blocks = TOKENS // TOK_DEV
    limit = jax.random.randint(key_limit, (blocks, 1), 5, 80)
    roll = jax.random.randint(key_roll, (blocks, TOK_DEV), 0, 100)
    wet = (roll >= limit).reshape(TOKENS)
    leading = jnp.arange(TOKENS) % REGION == 0
    return jnp.where(wet | leading, 1, 0).astype(jnp.int32)


def set_ends(values, rng, smallest, top_value):
    shape = values.shape
    spot = [jax.random.randint(jax.random.fold_in(rng, axis), (), 0, shape[axis]) for axis in range(len(shape))]
    values = values.at[tuple(spot)].set(smallest)
    longest = shape.index(max(shape))
    spot[longest] = (spot[longest] + 1) % shape[longest]
    return values.at[tuple(spot)].set(top_value)


def steps_of(rng, extent, shards, least, high):
    def one(axis_at, parts):
        heights = jax.random.uniform(jax.random.fold_in(jax.random.fold_in(rng, 6), axis_at), (parts,), jnp.float32, least / len(shards), high / len(shards))
        return jnp.repeat(jnp.exp(heights), extent[axis_at] // parts).reshape((-1,) + (1,) * (len(extent) - axis_at - 1))

    level = one(*shards[0])
    for cut in shards[1:]:
        level = level * one(*cut)
    return level


def normal_values(stream_key, shape, spread, most, shards=(), held_as=jnp.bfloat16):
    values = spread * jax.random.normal(stream_key, shape, jnp.float32)
    if shards:
        values = values * steps_of(stream_key, shape, shards, -0.22, 0.18)
    return jnp.clip(values, -most, most).astype(held_as)


def setup_inputs(seed: int = 0) -> dict:
    streams_of = jax.random.split(jax.random.key(seed), 11)
    acts_in = draw_acts_in(jax.random.fold_in(streams_of[10], 71), 0)
    first_in = draw_first_in(jax.random.fold_in(streams_of[10], 71), 0)
    saved_one = draw_saved_one(jax.random.fold_in(streams_of[10], 71), 0)
    cot_one = normal_values(streams_of[3], (SECTIONS, TOKENS, D), 1.0, 6.0, ((0, 4), (1, 64)))
    saved_two = draw_saved_two(jax.random.fold_in(streams_of[10], 71), 0)
    cot_last = normal_values(streams_of[5], (TOKENS, D), 1.0, 6.0, ((0, 64),))
    gains = jnp.clip(1.0 + 0.18 * jax.random.normal(streams_of[6], (SECTIONS, 3, D), jnp.float32), 0.1, 1.9)
    slopes = jnp.clip(jnp.exp(math.log(0.5) - 5.115996 * jax.random.uniform(streams_of[7], (SECTIONS, HEADS), jnp.float32) ** steps_of(streams_of[7], (SECTIONS, HEADS), ((0, 4),), -0.2, 0.2)), 0.003, 0.5)
    ocean = draw_ocean(jax.random.fold_in(streams_of[10], 71), 0)
    places = set_ends(jax.random.randint(streams_of[9], (2, TOKENS), 0, 64), jax.random.fold_in(streams_of[9], 1), 0, 63).astype(jnp.int32)
    return {"acts_in": acts_in, "first_in": first_in, "saved_one": saved_one, "cot_one": cot_one, "saved_two": saved_two, "cot_last": cot_last, "gains": gains, "slopes": slopes, "ocean": ocean, "places": places}


def normed(hidden_wide):
    return hidden_wide * lax.rsqrt(lax.optimization_barrier(jnp.mean(hidden_wide * hidden_wide, axis=-1, keepdims=True)) + 1e-05)

def product(einsum_form, left, right):
    return jnp.einsum(einsum_form, left.astype(jnp.float32), right.astype(jnp.float32))

def probabilities(query_b, key_b, query_pos, key_pos, key_ocean, slope_vec):
    scores = product('bmhe,blhe->bhml', query_b, key_b) * query_b.shape[-1] ** (-0.5)
    distance = jnp.abs(query_pos[0][:, :, None] - key_pos[0][:, None, :]) + jnp.abs(query_pos[1][:, :, None] - key_pos[1][:, None, :])
    scores = scores - slope_vec[None, :, None, None] * distance.astype(jnp.float32)[:, None]
    scores = jnp.where(key_ocean[:, None, None, :] > 0, scores, -1e+30)
    row_max = lax.optimization_barrier(jnp.max(scores, axis=-1, keepdims=True))
    exps = jnp.exp(scores - row_max)
    return exps / lax.optimization_barrier(jnp.sum(exps, axis=-1, keepdims=True))

def through(probs, query_b, key_b, value_b, masked_b):
    grad_probs = product('bmhe,blhe->bhml', masked_b, value_b)
    grad_value = product('bhml,bmhe->blhe', probs.astype(jnp.bfloat16), masked_b)
    grad_scores = probs * (grad_probs - lax.optimization_barrier(jnp.sum(probs * grad_probs, axis=-1, keepdims=True)))
    scaled = (grad_scores * query_b.shape[-1] ** (-0.5)).astype(jnp.bfloat16)
    grad_query = product('bhml,blhe->bmhe', scaled, key_b)
    grad_key = product('bhml,bmhe->blhe', scaled, query_b)
    return (grad_query, grad_key, grad_value)

def section_parts(hidden_in, gain_rows):
    hidden_wide = hidden_in.astype(jnp.float32)
    normed_in = normed(hidden_wide).astype(jnp.bfloat16)
    normed_wide = normed_in.astype(jnp.float32)
    query_all = (normed_wide * gain_rows[0]).astype(jnp.bfloat16)
    key_all = (normed_wide * gain_rows[1]).astype(jnp.bfloat16)
    value_all = (normed_wide * gain_rows[2]).astype(jnp.bfloat16)
    return (hidden_wide, normed_wide, query_all, key_all, value_all)

def split_regions(matrix):
    return matrix.reshape(TOKENS // REGION, REGION, HEADS, HD)

def forward(hidden_in, gain_rows, slope_vec, ocean, places):
    hidden_wide, normed_wide, query_all, key_all, value_all = section_parts(hidden_in, gain_rows)
    region_pos = places.reshape(2, TOKENS // REGION, REGION).transpose(1, 0, 2)
    region_ocean = ocean.reshape(TOKENS // REGION, REGION)

    def region(region_item):
        query_b, key_b, value_b, pos_b, ocean_b = region_item
        probs = probabilities(query_b[None], key_b[None], pos_b[:, None], pos_b[:, None], ocean_b[None], slope_vec)
        return product('bhml,blhe->bmhe', probs.astype(jnp.bfloat16), value_b[None])[0].astype(jnp.bfloat16)
    attended = lax.map(region, (split_regions(query_all), split_regions(key_all), split_regions(value_all), region_pos, region_ocean))
    attended = attended.reshape(TOKENS, D)
    keep = ocean.astype(jnp.float32)[:, None]
    return (hidden_wide + keep * attended.astype(jnp.float32)).astype(jnp.bfloat16)

def backward(hidden_in, cot_in, gain_rows, slope_vec, ocean, places):
    hidden_wide, normed_wide, query_all, key_all, value_all = section_parts(hidden_in, gain_rows)
    keep = ocean.astype(jnp.float32)[:, None]
    cot_wide = cot_in.astype(jnp.float32)
    masked = (keep * cot_wide).astype(jnp.bfloat16)
    region_pos = places.reshape(2, TOKENS // REGION, REGION).transpose(1, 0, 2)
    region_ocean = ocean.reshape(TOKENS // REGION, REGION)

    def region(region_item):
        query_b, key_b, value_b, masked_b, pos_b, ocean_b = region_item
        probs = probabilities(query_b[None], key_b[None], pos_b[:, None], pos_b[:, None], ocean_b[None], slope_vec)
        grad_query, grad_key, grad_value = through(probs, query_b[None], key_b[None], value_b[None], masked_b[None])
        return (grad_query[0], grad_key[0], grad_value[0])
    grad_query, grad_key, grad_value = lax.map(region, (split_regions(query_all), split_regions(key_all), split_regions(value_all), split_regions(masked), region_pos, region_ocean))
    grad_query = grad_query.reshape(TOKENS, D)
    grad_key = grad_key.reshape(TOKENS, D)
    grad_value = grad_value.reshape(TOKENS, D)
    grad_normed = grad_query * gain_rows[0] + grad_key * gain_rows[1] + grad_value * gain_rows[2]
    gain_part = jnp.stack([lax.optimization_barrier(jnp.sum(grad_query * normed_wide, axis=0)), lax.optimization_barrier(jnp.sum(grad_key * normed_wide, axis=0)), lax.optimization_barrier(jnp.sum(grad_value * normed_wide, axis=0))])
    unused, pull_back = jax.vjp(normed, hidden_wide)
    grad_hidden = cot_wide + pull_back(grad_normed)[0]
    return (grad_hidden.astype(jnp.bfloat16), gain_part)

def reference(acts_in, first_in, saved_one, cot_one, saved_two, cot_last, gains, slopes, ocean, places):
    out_list = []
    back_list = []
    gain_list = []
    for section_index in range(SECTIONS):
        out_list.append(forward(acts_in[section_index], gains[section_index], slopes[section_index], ocean, places))
        grad_hidden, gain_part = backward(saved_one[section_index], cot_one[section_index], gains[section_index], slopes[section_index], ocean, places)
        back_list.append(grad_hidden)
        gain_list.append(gain_part)
    second_out = []
    second_back = []
    for section_index in range(SECTIONS):
        if section_index == 0:
            second_in = first_in
        else:
            second_in = out_list[section_index - 1]
        if section_index == SECTIONS - 1:
            second_cot = cot_last
        else:
            second_cot = back_list[section_index + 1]
        second_out.append(forward(second_in, gains[section_index], slopes[section_index], ocean, places))
        grad_hidden, gain_part = backward(saved_two[section_index], second_cot, gains[section_index], slopes[section_index], ocean, places)
        second_back.append(grad_hidden)
        gain_list[section_index] = gain_list[section_index] + gain_part
    return (jnp.stack(out_list), jnp.stack(back_list), jnp.stack(second_out), jnp.stack(second_back), jnp.stack(gain_list))
```

```python
import functools

import jax
import jax.numpy as jnp
from jax import lax
from jax.experimental import pallas as pl
from jax.experimental.pallas import tpu as pltpu
from jax.sharding import PartitionSpec as P

D = 4096
HEADS = 32
HD = 128
REGION = 256
OWN = 128
HALF = D // 2
LOG2E = 1.4426950408889634
SCALE = HD ** (-0.5)
FAR = 1e30
STEP_HEADS = 4
VMEM_LIMIT = 48 * 1024 * 1024


def dot(left, right, left_dim, right_dim):
    return lax.dot_general(
        left,
        right,
        (((left_dim,), (right_dim,)), ((), ())),
        preferred_element_type=jnp.float32,
    )


def rows_of(own_ref, other_ref, cols):
    return jnp.concatenate([own_ref[:, cols], other_ref[:, cols]], axis=0).astype(jnp.float32)


def forward_body(
    query_rows, heads, own_ref, other_ref, inverse_ref, gains_ref, slopes_ref, table_ref, keep_ref, *out_refs
):
    step = pl.program_id(0)
    inverse = inverse_ref[...]
    keep = keep_ref[:query_rows]
    ones = jnp.ones((REGION, HD), jnp.bfloat16)
    for head in range(heads):
        cols = pl.ds(head * HD, HD)
        gains = gains_ref[:, cols]
        hidden = rows_of(own_ref, other_ref, cols)
        normed_in = (hidden * inverse).astype(jnp.bfloat16).astype(jnp.float32)
        query = (normed_in[:query_rows] * gains[0:1]).astype(jnp.bfloat16)
        key = (normed_in * gains[1:2]).astype(jnp.bfloat16)
        value = (normed_in * gains[2:3]).astype(jnp.bfloat16)
        slope = slopes_ref[0, step * heads + head] * LOG2E
        scores = dot(query, key, 1, 1) * (SCALE * LOG2E) - slope * table_ref[:query_rows]
        exps = jnp.exp2(scores - jnp.max(scores, axis=1, keepdims=True)).astype(jnp.bfloat16)
        mixed = dot(exps, jnp.concatenate([value, ones], axis=1), 1, 0)
        attended = (mixed[:, :HD] / mixed[:, HD:]).astype(jnp.bfloat16).astype(jnp.float32)
        result = (hidden[:query_rows] + keep * attended).astype(jnp.bfloat16)
        out_refs[0][:, cols] = result[:OWN]
        if query_rows == REGION:
            out_refs[1][:, cols] = result[OWN:]


def forward(query_rows, own, other, inverse, gains, slopes, table, keep):
    width = STEP_HEADS * HD
    wide = pl.BlockSpec((OWN, width), lambda j: (0, j))
    whole = lambda shape: pl.BlockSpec(shape, lambda j: (0, 0))
    outs = query_rows // OWN
    return pl.pallas_call(
        functools.partial(forward_body, query_rows, STEP_HEADS),
        grid=(D // width,),
        in_specs=[
            wide,
            wide,
            whole((REGION, 1)),
            pl.BlockSpec((3, width), lambda j: (0, j)),
            pl.BlockSpec(memory_space=pltpu.SMEM),
            whole((REGION, REGION)),
            whole((REGION, 1)),
        ],
        out_specs=[wide] * outs,
        out_shape=[jax.ShapeDtypeStruct((OWN, D), jnp.bfloat16)] * outs,
        compiler_params=pltpu.CompilerParams(vmem_limit_bytes=VMEM_LIMIT),
        cost_estimate=pl.CostEstimate(
            flops=4 * query_rows * REGION * D,
            bytes_accessed=4 * OWN * D * (1 + outs),
            transcendentals=query_rows * REGION * HEADS,
        ),
        name="attend" + str(query_rows),
    )(own, other, inverse, gains, slopes, table, keep)


def backward_body(
    heads,
    side_ref,
    own_ref,
    other_ref,
    cot_own_ref,
    cot_other_ref,
    inverse_ref,
    gains_ref,
    slopes_ref,
    table_ref,
    keep_ref,
    grad_ref,
    gain_ref,
    moment_ref,
    total_ref,
):
    step = pl.program_id(0)
    first_head = side_ref[0] * (HEADS // 2) + step * heads
    inverse = inverse_ref[...]
    keep = keep_ref[...]

    @pl.when(step == 0)
    def _():
        total_ref[...] = jnp.zeros_like(total_ref)

    for head in range(heads):
        cols = pl.ds(head * HD, HD)
        gains = gains_ref[:, cols]
        wide = rows_of(own_ref, other_ref, cols) * inverse
        normed_in = wide.astype(jnp.bfloat16).astype(jnp.float32)
        query = (normed_in * gains[0:1]).astype(jnp.bfloat16)
        key = (normed_in * gains[1:2]).astype(jnp.bfloat16)
        value = (normed_in * gains[2:3]).astype(jnp.bfloat16)
        masked = (rows_of(cot_own_ref, cot_other_ref, cols) * keep).astype(jnp.bfloat16)
        slope = slopes_ref[0, first_head + head] * LOG2E
        scores = dot(key, query, 1, 1) * (SCALE * LOG2E) - slope * table_ref[...]
        exps = jnp.exp2(scores - jnp.max(scores, axis=0, keepdims=True))
        probs = exps * (1.0 / jnp.sum(exps, axis=0, keepdims=True))
        grad_probs = dot(value, masked, 1, 1)
        inner = jnp.sum(probs * grad_probs, axis=0, keepdims=True)
        grad_scores = (probs * (grad_probs - inner) * SCALE).astype(jnp.bfloat16)
        grad_value = dot(probs.astype(jnp.bfloat16), masked, 1, 0)
        grad_key = dot(grad_scores, query, 1, 0)
        grad_query = dot(grad_scores, key, 0, 0)
        grad = grad_query * gains[0:1] + grad_key * gains[1:2] + grad_value * gains[2:3]
        grad_ref[:, cols] = grad
        total_ref[...] += grad * wide
        gain_ref[0:1, cols] = jnp.sum(grad_query * normed_in, axis=0, keepdims=True)
        gain_ref[1:2, cols] = jnp.sum(grad_key * normed_in, axis=0, keepdims=True)
        gain_ref[2:3, cols] = jnp.sum(grad_value * normed_in, axis=0, keepdims=True)

    @pl.when(step == pl.num_programs(0) - 1)
    def _():
        moment_ref[...] = jnp.sum(total_ref[...], axis=1, keepdims=True)


def backward(side, own, other, cot_own, cot_other, inverse, gains, slopes, table, keep):
    width = STEP_HEADS * HD
    steps = HALF // width
    half = pl.BlockSpec((OWN, width), lambda j, s: (0, j))

    def block(array):
        if array.shape[1] == HALF:
            return half
        return pl.BlockSpec((array.shape[0], width), lambda j, s: (0, s[0] * steps + j))

    whole = lambda shape: pl.BlockSpec(shape, lambda j, s: (0, 0))
    return pl.pallas_call(
        functools.partial(backward_body, STEP_HEADS),
        grid_spec=pltpu.PrefetchScalarGridSpec(
            num_scalar_prefetch=1,
            grid=(steps,),
            in_specs=[
                block(own),
                block(other),
                block(cot_own),
                block(cot_other),
                whole((REGION, 1)),
                block(gains),
                pl.BlockSpec(memory_space=pltpu.SMEM),
                whole((REGION, REGION)),
                whole((REGION, 1)),
            ],
            out_specs=[
                pl.BlockSpec((REGION, width), lambda j, s: (0, j)),
                pl.BlockSpec((3, width), lambda j, s: (0, j)),
                whole((REGION, 1)),
            ],
            scratch_shapes=[pltpu.VMEM((REGION, HD), jnp.float32)],
        ),
        out_shape=[
            jax.ShapeDtypeStruct((REGION, HALF), jnp.float32),
            jax.ShapeDtypeStruct((3, HALF), jnp.float32),
            jax.ShapeDtypeStruct((REGION, 1), jnp.float32),
        ],
        compiler_params=pltpu.CompilerParams(vmem_limit_bytes=VMEM_LIMIT),
        cost_estimate=pl.CostEstimate(
            flops=10 * REGION * REGION * HALF,
            bytes_accessed=4 * REGION * HALF + 4 * REGION * HALF,
            transcendentals=REGION * REGION * HEADS // 2,
        ),
        name="differentiate",
    )(side, own, other, cot_own, cot_other, inverse, gains, slopes, table, keep)


def combine_body(
    side_ref, own_ref, other_ref, cot_own_ref, cot_other_ref, grad_ref, inverse_ref, moment_ref, out_own, out_other
):
    inverse = inverse_ref[...]
    mean = moment_ref[...] * (1.0 / D)
    for rows, hidden, cot, out in (
        (slice(0, OWN), own_ref, cot_own_ref, out_own),
        (slice(OWN, REGION), other_ref, cot_other_ref, out_other),
    ):
        scale = inverse[rows]
        wide = hidden[...].astype(jnp.float32) * scale
        grad = (grad_ref[rows] - wide * mean[rows]) * scale
        out[...] = (cot[...].astype(jnp.float32) + grad).astype(jnp.bfloat16)


def combine(side, own, other, cot_own, cot_other, grad, inverse, moment):
    width = STEP_HEADS * HD
    steps = HALF // width
    half = pl.BlockSpec((OWN, width), lambda j, s: (0, j))

    def block(array):
        if array.shape[1] == HALF:
            return half
        return pl.BlockSpec((array.shape[0], width), lambda j, s: (0, s[0] * steps + j))

    whole = pl.BlockSpec((REGION, 1), lambda j, s: (0, 0))
    return pl.pallas_call(
        combine_body,
        grid_spec=pltpu.PrefetchScalarGridSpec(
            num_scalar_prefetch=1,
            grid=(steps,),
            in_specs=[
                block(own),
                block(other),
                block(cot_own),
                block(cot_other),
                pl.BlockSpec((REGION, width), lambda j, s: (0, j)),
                whole,
                whole,
            ],
            out_specs=[half, half],
        ),
        out_shape=[jax.ShapeDtypeStruct((OWN, HALF), jnp.bfloat16)] * 2,
        compiler_params=pltpu.CompilerParams(vmem_limit_bytes=VMEM_LIMIT),
        cost_estimate=pl.CostEstimate(
            flops=6 * REGION * HALF, bytes_accessed=10 * REGION * HALF, transcendentals=0
        ),
        name="combine",
    )(side, own, other, cot_own, cot_other, grad, inverse, moment)


def after(value, *earlier):
    return lax.optimization_barrier((value, earlier))[0]


def inverse_norm(hidden):
    wide = hidden.astype(jnp.float32)
    return lax.rsqrt(jnp.mean(wide * wide, axis=1, keepdims=True) + 1e-05)


def on_device(
    acts_in, first_in, saved_one, cot_one, saved_two, cot_last, gains, slopes, ocean, places
):
    devices = lax.axis_size("seq")
    sections = lax.axis_size("section")
    my_index = lax.axis_index("seq")
    section_index = lax.axis_index("section")
    side = my_index % 2
    side_vec = side.astype(jnp.int32)[None]
    acts, saved_a, cot_a, saved_b = (acts_in[0], saved_one[0], cot_one[0], saved_two[0])
    gain_rows = gains[0]
    partners = [(i, i ^ 1) for i in range(devices)]

    def swap(value):
        return lax.ppermute(value, "seq", partners)

    def swap_in(section, value):
        base = section * devices
        return lax.ppermute(
            value, ("section", "seq"), [(base + i, base + (i ^ 1)) for i in range(devices)]
        )

    def shifted(value, steps):
        first, last = (max(0, -steps), min(sections, sections - steps))
        return lax.ppermute(value, "section", [(s, s + steps) for s in range(first, last)])

    def for_partner(matrix):
        return lax.dynamic_slice_in_dim(matrix, (1 - side) * HALF, HALF, 1)

    def for_me(matrix):
        return lax.dynamic_slice_in_dim(matrix, side * HALF, HALF, 1)

    def joined(mine, received):
        pair = jnp.concatenate([mine, received], axis=1)
        flipped = jnp.concatenate([received, mine], axis=1)
        return jnp.where(side == 0, pair, flipped)

    def whole_rows(moment):
        received = swap(moment)
        return moment + jnp.concatenate([received[OWN:], received[:OWN]], axis=0)

    def region_order(vector):
        own = lax.dynamic_slice_in_dim(vector, my_index * OWN, OWN, vector.ndim - 1)
        start = (my_index + 1 - 2 * side) * OWN
        other = lax.dynamic_slice_in_dim(vector, start, OWN, vector.ndim - 1)
        return jnp.concatenate([own, other], axis=-1)

    place = region_order(places)
    wet = region_order(ocean)
    distance = (
        jnp.abs(place[0][:, None] - place[0][None, :])
        + jnp.abs(place[1][:, None] - place[1][None, :])
    ).astype(jnp.float32)
    by_query = jnp.where(wet[None, :] > 0, distance, FAR)
    by_key = jnp.where(wet[:, None] > 0, distance, FAR)
    keep = wet.astype(jnp.float32)[:, None]

    saved_a_other = swap(for_partner(saved_a))
    cot_a_other = swap(for_partner(cot_a))
    own_inverse = jnp.concatenate([inverse_norm(saved_a), inverse_norm(saved_b)], axis=1)
    other_inverse = swap(own_inverse)
    inverse_ab = jnp.concatenate([own_inverse, other_inverse], axis=0)
    inverse_a, inverse_b = (inverse_ab[:, 0:1], inverse_ab[:, 1:2])

    saved_b_send = after(for_partner(saved_b), saved_a_other)
    saved_b_other = swap(saved_b_send)
    cot_last_other = swap_in(sections - 1, after(for_partner(cot_last), saved_a_other))
    acts_other = swap(after(acts, saved_b_other))

    back = (side_vec, saved_a, saved_a_other, cot_a, cot_a_other)
    grad, gain_a, moment = backward(*back, inverse_a, gain_rows, slopes, by_key, keep)
    moment = whole_rows(moment)
    first_own, first_other = combine(*back, grad, inverse_a, moment)
    grad_one_part = swap(after(first_other, acts_other))
    next_own, next_other = (shifted(first_own, -1), shifted(first_other, -1))

    is_last = section_index == sections - 1
    cot_b_own = jnp.where(is_last, for_me(cot_last), next_own)
    cot_b_other = jnp.where(is_last, cot_last_other, next_other)
    back = (side_vec, saved_b, saved_b_other, cot_b_own, cot_b_other)
    grad, gain_b, moment = backward(*back, inverse_b, gain_rows, slopes, by_key, keep)
    moment = whole_rows(moment)
    second_own, second_other = combine(*back, grad, inverse_b, moment)
    bwd_two_part = swap(after(second_other, acts_other))

    first_in_other = swap_in(0, after(first_in, acts_other))

    gain = gain_a + gain_b
    bit = 2
    while bit < devices:
        terms = [gain]
        for flip in ([bit] if bit == 2 else [bit, 2 * bit, 3 * bit]):
            terms.append(lax.ppermute(gain, "seq", [(i, i ^ flip) for i in range(devices)]))
        if bit == 2:
            gain = terms[0] + terms[1]
            bit = 4
        else:
            gain = (terms[0] + terms[1]) + (terms[2] + terms[3])
            bit = 4 * bit
    gain_total = joined(gain, swap(gain))

    inverse = jnp.concatenate([inverse_norm(acts), inverse_norm(acts_other)], axis=0)
    out_own, out_other = forward(
        REGION, acts, acts_other, inverse, gain_rows, slopes, by_query, keep
    )
    is_first = section_index == 0
    in_own = jnp.where(is_first, first_in, shifted(out_own, 1))
    in_other = jnp.where(is_first, first_in_other, shifted(out_other, 1))
    inverse = jnp.concatenate([inverse_norm(in_own), inverse_norm(in_other)], axis=0)
    (fwd_two,) = forward(OWN, in_own, in_other, inverse, gain_rows, slopes, by_query, keep)

    grad_one = joined(first_own, grad_one_part)
    bwd_two = joined(second_own, bwd_two_part)
    return (out_own[None], grad_one[None], fwd_two[None], bwd_two[None], gain_total[None])


def solution(mesh):
    placed = (
        P("section", "seq", None),
        P("seq", None),
        P("section", "seq", None),
        P("section", "seq", None),
        P("section", "seq", None),
        P("seq", None),
        P("section", None, None),
        P("section", None),
        P(),
        P(),
    )
    return jax.shard_map(
        on_device,
        mesh=mesh,
        in_specs=placed,
        out_specs=(
            P("section", "seq", None),
            P("section", "seq", None),
            P("section", "seq", None),
            P("section", "seq", None),
            P("section", None, None),
        ),
        check_vma=False,
    )
```

```python
import functools

import jax
import jax.numpy as jnp
from jax import lax
from jax.experimental import pallas as pl
from jax.experimental.pallas import tpu as pltpu
from jax.sharding import PartitionSpec as P

D = 4096
HEADS = 32
HD = 128
REGION = 256
OWN = 128
HALF = D // 2
LATE = 3 * D // 4
LOG2E = 1.4426950408889634
SCALE = HD ** (-0.5)
FAR = 1e30
STEP_HEADS = 4
VMEM_LIMIT = 16 * 1024 * 1024
FREE = pl.CostEstimate(flops=0, bytes_accessed=0, transcendentals=0)


def dot(left, right, left_dim, right_dim):
    return lax.dot_general(
        left,
        right,
        (((left_dim,), (right_dim,)), ((), ())),
        preferred_element_type=jnp.float32,
    )


def columns_of(rows_ref, out_ref):
    for part in range(2):
        row = jnp.broadcast_to(rows_ref[part : part + 1, :OWN], (OWN, OWN))
        out_ref[part * OWN : (part + 1) * OWN] = jnp.transpose(row)


def split_columns(refs, out_ref):
    for part, ref in enumerate(refs):
        pieces = ref[:, 0:3].astype(jnp.float32)
        column = (pieces[:, 0:1] + pieces[:, 1:2]) + pieces[:, 2:3]
        out_ref[part * OWN : (part + 1) * OWN] = jnp.broadcast_to(column, (OWN, HD))


def rows_of(own_ref, other_ref, cols):
    return jnp.concatenate([own_ref[:, cols], other_ref[:, cols]], axis=0).astype(jnp.float32)


def row_block(array, part, width, column):
    row = part if array.shape[0] == REGION else 0
    return pl.BlockSpec((OWN, width), lambda j, *s: (row, column(j, *s)))


def whole(shape):
    return pl.BlockSpec(shape, lambda j, *s: (0, 0))


def forward_body(
    query_rows, heads, own_ref, other_ref, inverse_ref, gains_ref, slopes_ref, table_ref, keep_ref, *refs
):
    *out_refs, column_ref = refs
    step = pl.program_id(0)

    @pl.when(step == 0)
    def _():
        columns_of(inverse_ref, column_ref)

    inverse = column_ref[...]
    keep = keep_ref[:query_rows]
    ones = jnp.ones((REGION, HD), jnp.bfloat16)
    for head in range(heads):
        cols = pl.ds(head * HD, HD)
        gains = gains_ref[:, cols]
        hidden = rows_of(own_ref, other_ref, cols)
        normed_in = (hidden * inverse).astype(jnp.bfloat16).astype(jnp.float32)
        query = (normed_in[:query_rows] * gains[0:1]).astype(jnp.bfloat16)
        key = (normed_in * gains[1:2]).astype(jnp.bfloat16)
        value = (normed_in * gains[2:3]).astype(jnp.bfloat16)
        slope = slopes_ref[0, step * heads + head] * LOG2E
        scores = dot(query, key, 1, 1) * (SCALE * LOG2E) - slope * table_ref[:query_rows]
        exps = jnp.exp2(scores - jnp.max(scores, axis=1, keepdims=True)).astype(jnp.bfloat16)
        mixed = dot(exps, jnp.concatenate([value, ones], axis=1), 1, 0)
        attended = (mixed[:, :HD] / mixed[:, HD:]).astype(jnp.bfloat16).astype(jnp.float32)
        result = (hidden[:query_rows] + keep * attended).astype(jnp.bfloat16)
        out_refs[0][:, cols] = result[:OWN]
        if query_rows == REGION:
            out_refs[1][:, cols] = result


def forward(query_rows, own, other, inverse, gains, slopes, table, keep):
    width = STEP_HEADS * HD
    column = lambda j: j
    rows = [OWN] if query_rows == OWN else [OWN, REGION]
    return pl.pallas_call(
        functools.partial(forward_body, query_rows, STEP_HEADS),
        grid=(D // width,),
        in_specs=[
            row_block(own, 0, width, column),
            row_block(other, 1, width, column),
            whole((2, OWN)),
            pl.BlockSpec((3, width), lambda j: (0, j)),
            pl.BlockSpec(memory_space=pltpu.SMEM),
            whole((REGION, REGION)),
            whole((REGION, 1)),
        ],
        out_specs=[pl.BlockSpec((count, width), lambda j: (0, j)) for count in rows],
        out_shape=[jax.ShapeDtypeStruct((count, D), jnp.bfloat16) for count in rows],
        scratch_shapes=[pltpu.VMEM((REGION, HD), jnp.float32)],
        compiler_params=pltpu.CompilerParams(vmem_limit_bytes=VMEM_LIMIT),
        cost_estimate=FREE,
        name="attend" + str(query_rows),
    )(own, other, inverse, gains, slopes, table, keep)


def half_blocks(steps, width, *arrays):
    here = lambda j, s: j
    within = lambda j, s: s[0] * steps + j
    return [
        row_block(array, place % 2, width, within if array.shape[1] == D else here)
        for place, array in enumerate(arrays)
    ]


def tail_blocks():
    return [pl.BlockSpec((OWN, HD), lambda j, s: (0, HALF // HD))] * 2


def backward_body(
    heads,
    side_ref,
    own_ref,
    other_ref,
    cot_own_ref,
    cot_other_ref,
    inverse_own_ref,
    inverse_other_ref,
    gains_ref,
    slopes_ref,
    table_ref,
    keep_ref,
    grad_ref,
    small_ref,
    total_ref,
    column_ref,
):
    step = pl.program_id(0)
    first_head = side_ref[0] * (HEADS // 2) + step * heads
    keep = keep_ref[...]

    @pl.when(step == 0)
    def _():
        total_ref[...] = jnp.zeros_like(total_ref)
        small_ref[...] = jnp.zeros_like(small_ref)
        split_columns((inverse_own_ref, inverse_other_ref), column_ref)

    inverse = column_ref[...]

    for head in range(heads):
        cols = pl.ds(head * HD, HD)
        gains = gains_ref[:, cols]
        wide = rows_of(own_ref, other_ref, cols) * inverse
        normed_in = wide.astype(jnp.bfloat16).astype(jnp.float32)
        query = (normed_in * gains[0:1]).astype(jnp.bfloat16)
        key = (normed_in * gains[1:2]).astype(jnp.bfloat16)
        value = (normed_in * gains[2:3]).astype(jnp.bfloat16)
        masked = (rows_of(cot_own_ref, cot_other_ref, cols) * keep).astype(jnp.bfloat16)
        slope = slopes_ref[0, first_head + head] * LOG2E
        scores = dot(key, query, 1, 1) * (SCALE * LOG2E) - slope * table_ref[...]
        exps = jnp.exp2(scores - jnp.max(scores, axis=0, keepdims=True))
        probs = exps * (1.0 / jnp.sum(exps, axis=0, keepdims=True))
        grad_probs = dot(value, masked, 1, 1)
        inner = jnp.sum(probs * grad_probs, axis=0, keepdims=True)
        grad_scores = (probs * (grad_probs - inner) * SCALE).astype(jnp.bfloat16)
        grad_value = dot(probs.astype(jnp.bfloat16), masked, 1, 0)
        grad_key = dot(grad_scores, query, 1, 0)
        grad_query = dot(grad_scores, key, 0, 0)
        grad = grad_query * gains[0:1] + grad_key * gains[1:2] + grad_value * gains[2:3]
        grad_ref[:, cols] = grad
        total_ref[...] += grad * wide
        small_ref[0:1, pl.ds((step * heads + head) * HD, HD)] = jnp.sum(grad_query * normed_in, axis=0, keepdims=True)
        small_ref[1:2, pl.ds((step * heads + head) * HD, HD)] = jnp.sum(grad_key * normed_in, axis=0, keepdims=True)
        small_ref[2:3, pl.ds((step * heads + head) * HD, HD)] = jnp.sum(grad_value * normed_in, axis=0, keepdims=True)

    @pl.when(step == pl.num_programs(0) - 1)
    def _():
        moment = lax.dot_general(
            jnp.ones((8, HD), jnp.float32),
            total_ref[...],
            (((1,), (1,)), ((), ())),
            precision=lax.Precision.HIGHEST,
            preferred_element_type=jnp.float32,
        )
        small_ref[3:4, :REGION] = moment[0:1]


def backward(side, own, sent, other, cot_own, cot_other, gains, slopes, table, keep):
    width = STEP_HEADS * HD
    steps = HALF // width
    return pl.pallas_call(
        functools.partial(backward_body, STEP_HEADS),
        grid_spec=pltpu.PrefetchScalarGridSpec(
            num_scalar_prefetch=1,
            grid=(steps,),
            in_specs=[
                *half_blocks(steps, width, own, other, cot_own, cot_other),
                *tail_blocks(),
                pl.BlockSpec((3, width), lambda j, s: (0, s[0] * steps + j)),
                pl.BlockSpec(memory_space=pltpu.SMEM),
                whole((REGION, REGION)),
                whole((REGION, 1)),
            ],
            out_specs=[pl.BlockSpec((REGION, width), lambda j, s: (0, j)), whole((4, HALF))],
            scratch_shapes=[pltpu.VMEM((REGION, HD), jnp.float32)] * 2,
        ),
        out_shape=[
            jax.ShapeDtypeStruct((REGION, HALF), jnp.float32),
            jax.ShapeDtypeStruct((4, HALF), jnp.float32),
        ],
        compiler_params=pltpu.CompilerParams(vmem_limit_bytes=VMEM_LIMIT),
        cost_estimate=FREE,
        name="differentiate",
    )(side, own, other, cot_own, cot_other, sent, other, gains, slopes, table, keep)


def combine_body(
    side_ref,
    own_ref,
    other_ref,
    cot_own_ref,
    cot_other_ref,
    grad_ref,
    inverse_own_ref,
    inverse_other_ref,
    small_ref,
    received_ref,
    out_ref,
    out_other,
    column_ref,
    mean_ref,
):
    @pl.when(pl.program_id(0) == 0)
    def _():
        split_columns((inverse_own_ref, inverse_other_ref), column_ref)
        for part in range(2):
            here, there = (pl.ds(part * OWN, OWN), pl.ds((1 - part) * OWN, OWN))
            total = small_ref[3:4, here] + received_ref[3:4, there]
            mean_ref[here] = jnp.transpose(jnp.broadcast_to(total, (OWN, OWN))) * (1.0 / D)

    for part, hidden, cot in ((0, own_ref, cot_own_ref), (1, other_ref, cot_other_ref)):
        rows = pl.ds(part * OWN, OWN)
        scale = column_ref[rows]
        mean = mean_ref[rows]
        for piece in range(out_ref.shape[1] // HD):
            cols = pl.ds(piece * HD, HD)
            wide = hidden[:, cols].astype(jnp.float32) * scale
            grad = (grad_ref[rows, cols] - wide * mean) * scale
            result = (cot[:, cols].astype(jnp.float32) + grad).astype(jnp.bfloat16)
            out_ref[rows, cols] = result
            if part == 1:
                out_other[:, cols] = result


def combine(side, own, sent, other, cot_own, cot_other, grad, small, received):
    width = STEP_HEADS * HD
    steps = HALF // width
    return pl.pallas_call(
        combine_body,
        grid_spec=pltpu.PrefetchScalarGridSpec(
            num_scalar_prefetch=1,
            grid=(steps,),
            in_specs=[
                *half_blocks(steps, width, own, other, cot_own, cot_other),
                pl.BlockSpec((REGION, width), lambda j, s: (0, j)),
                *tail_blocks(),
                whole((4, HALF)),
                whole((4, HALF)),
            ],
            out_specs=[
                pl.BlockSpec((count, width), lambda j, s: (0, j)) for count in (REGION, OWN)
            ],
            scratch_shapes=[pltpu.VMEM((REGION, HD), jnp.float32)] * 2,
        ),
        out_shape=[
            jax.ShapeDtypeStruct((count, HALF), jnp.bfloat16) for count in (REGION, OWN)
        ],
        compiler_params=pltpu.CompilerParams(vmem_limit_bytes=VMEM_LIMIT),
        cost_estimate=FREE,
        name="combine",
    )(side, own, other, cot_own, cot_other, grad, sent, other, small, received)


def after(value, *earlier):
    return lax.optimization_barrier((value, earlier))[0]


def with_inverse(half, inverse):
    first = lax.reduce_precision(inverse, 8, 7)
    second = lax.reduce_precision(inverse - first, 8, 7)
    pieces = jnp.stack([first, second, inverse - first - second], axis=1).astype(jnp.bfloat16)
    return jnp.concatenate([half, jnp.pad(pieces, ((0, 0), (0, HD - 3)))], axis=1)


def inverse_norm(hidden):
    wide = hidden.astype(jnp.float32)
    return lax.rsqrt(jnp.mean(wide * wide, axis=1) + 1e-05)


def on_device(
    acts_in, first_in, saved_one, cot_one, saved_two, cot_last, gains, slopes, ocean, places
):
    devices = lax.axis_size("seq")
    sections = lax.axis_size("section")
    my_index = lax.axis_index("seq")
    section_index = lax.axis_index("section")
    side = my_index % 2
    side_vec = side.astype(jnp.int32)[None]
    acts, saved_a, cot_a, saved_b = (acts_in[0], saved_one[0], cot_one[0], saved_two[0])
    gain_rows = gains[0]

    def flips(bits):
        return [(i, i ^ bits) for i in range(devices)]

    def swap(value):
        return lax.ppermute(value, "seq", flips(1))

    def swap_in(chosen, value):
        bases = [section * devices for section in chosen]
        pairs = [(base + i, base + (i ^ 1)) for base in bases for i in range(devices)]
        return lax.ppermute(value, ("section", "seq"), pairs)

    def shifted(value, steps):
        first, last = (max(0, -steps), min(sections, sections - steps))
        return lax.ppermute(value, "section", [(s, s + steps) for s in range(first, last)])

    def for_partner(matrix):
        return lax.dynamic_slice_in_dim(matrix, (1 - side) * HALF, HALF, 1)

    def for_me(matrix):
        return lax.dynamic_slice_in_dim(matrix, side * HALF, HALF, 1)

    def joined(mine, received):
        pair = jnp.concatenate([mine, received], axis=1)
        flipped = jnp.concatenate([received, mine], axis=1)
        return jnp.where(side == 0, pair, flipped)

    def region_order(vector):
        own = lax.dynamic_slice_in_dim(vector, my_index * OWN, OWN, vector.ndim - 1)
        start = (my_index + 1 - 2 * side) * OWN
        other = lax.dynamic_slice_in_dim(vector, start, OWN, vector.ndim - 1)
        return jnp.concatenate([own, other], axis=-1)

    place = region_order(places)
    wet = region_order(ocean)
    distance = (
        jnp.abs(place[0][:, None] - place[0][None, :])
        + jnp.abs(place[1][:, None] - place[1][None, :])
    ).astype(jnp.float32)
    by_query = jnp.where(wet[None, :] > 0, distance, FAR)
    by_key = jnp.where(wet[:, None] > 0, distance, FAR)
    keep = wet.astype(jnp.float32)[:, None]

    is_first = section_index == 0
    is_last = section_index == sections - 1

    with jax.named_scope("cot_a"):
        cot_a_send = for_partner(cot_a)
        cot_a_other = swap(cot_a_send)
    with jax.named_scope("saved_a"):
        early = after(saved_a, cot_a_send)
        saved_a_sent = with_inverse(for_partner(early), inverse_norm(early))
        saved_a_other = swap(saved_a_sent)
    saved_b_sent = with_inverse(for_partner(saved_b), inverse_norm(after(saved_b, saved_a_sent)))
    with jax.named_scope("acts"):
        acts_other = swap(after(acts, saved_a_other))

    back = (side_vec, saved_a, saved_a_sent, saved_a_other, cot_a, cot_a_other)
    grad, small_a = backward(*back, gain_rows, slopes, by_key, keep)
    with jax.named_scope("small_a"):
        received_a = swap(small_a)
    received_a = after(received_a, acts_other)
    first, first_other = combine(*back, grad, small_a, received_a)
    with jax.named_scope("to_previous"):
        from_next = shifted(first, -1)
    with jax.named_scope("saved_b"):
        saved_b_other = swap(after(saved_b_sent, acts_other))
    with jax.named_scope("extra"):
        extra = jnp.concatenate([first_in[:, LATE:], for_partner(cot_last)], axis=1)
        extra = jnp.where(is_last, extra, first_in[:, :LATE])
        received_extra = swap_in((sections - 2, sections - 1), after(extra, acts_other))
    with jax.named_scope("helped"):
        early_part = lax.ppermute(received_extra, "section", [(sections - 2, 0)])
        late_part = lax.ppermute(received_extra[:, : D - LATE], "section", [(sections - 1, 0)])

    acts_other = after(acts_other, first)
    inverse = jnp.stack([inverse_norm(acts), inverse_norm(acts_other)])
    out_one, out_region = forward(
        REGION, acts, acts_other, inverse, gain_rows, slopes, by_query, keep
    )
    with jax.named_scope("to_next"):
        from_before = shifted(out_region, 1)
    with jax.named_scope("grad_one"):
        grad_one_part = swap(after(first_other, saved_b_other))

    cot_b = jnp.concatenate([for_me(cot_last), received_extra[:, D - LATE :]], axis=0)
    cot_b = after(jnp.where(is_last, cot_b, from_next), out_one)
    back = (side_vec, saved_b, saved_b_sent, saved_b_other, cot_b, cot_b)
    grad, small_b = backward(*back, gain_rows, slopes, by_key, keep)
    small = small_b + jnp.where(jnp.arange(4)[:, None] < 3, small_a, 0.0)
    with jax.named_scope("small_b"):
        received_b = swap(small)
    received_b = after(received_b, grad_one_part, early_part, late_part)
    gain_total = joined(small[:3], received_b[:3])
    received_b = after(received_b, gain_total)
    second, second_other = combine(*back, grad, small, received_b)
    with jax.named_scope("bwd_two"):
        bwd_two_part = swap(second_other)

    fed = jnp.concatenate([after(early_part, second_other), late_part], axis=1)
    fed = jnp.concatenate([first_in, fed], axis=0)
    region_in = jnp.where(is_first, fed, from_before)
    inverse = inverse_norm(region_in).reshape(2, OWN)
    (fwd_two,) = forward(OWN, region_in, region_in, inverse, gain_rows, slopes, by_query, keep)

    if devices > 2:
        with jax.named_scope("gain2"):
            gain_total = gain_total + lax.ppermute(gain_total, "seq", flips(2))
    gain_total = after(gain_total, from_before)
    for bit in (4, 16):
        if bit < devices:
            with jax.named_scope("gain" + str(bit)):
                terms = [
                    lax.ppermute(gain_total, "seq", flips(bit * flip)) for flip in range(1, 4)
                ]
            gain_total = (gain_total + terms[0]) + (terms[1] + terms[2])

    bwd_two_part = after(bwd_two_part, fwd_two, gain_total)

    grad_one = joined(first[:OWN], after(grad_one_part, second_other))
    bwd_two = joined(second[:OWN], bwd_two_part)
    return (out_one[None], grad_one[None], fwd_two[None], bwd_two[None], gain_total[None])


def solution(mesh):
    placed = (
        P("section", "seq", None),
        P("seq", None),
        P("section", "seq", None),
        P("section", "seq", None),
        P("section", "seq", None),
        P("seq", None),
        P("section", None, None),
        P("section", None),
        P(),
        P(),
    )
    return jax.shard_map(
        on_device,
        mesh=mesh,
        in_specs=placed,
        out_specs=(
            P("section", "seq", None),
            P("section", "seq", None),
            P("section", "seq", None),
            P("section", "seq", None),
            P("section", None, None),
        ),
        check_vma=False,
    )
```

```python
import functools

import jax
import jax.numpy as jnp
from jax import lax
from jax.experimental import pallas as pl
from jax.experimental.pallas import tpu as pltpu
from jax.sharding import PartitionSpec as P

D = 4096
HEADS = 32
HD = 128
REGION = 256
OWN = 128
HALF = D // 2
LATE = 3 * D // 4
LOG2E = 1.4426950408889634
SCALE = HD ** (-0.5)
FAR = 1e30
STEP_HEADS = 4
VMEM_LIMIT = 16 * 1024 * 1024
FREE = pl.CostEstimate(flops=0, bytes_accessed=0, transcendentals=0)


def dot(left, right, left_dim, right_dim):
    return lax.dot_general(
        left,
        right,
        (((left_dim,), (right_dim,)), ((), ())),
        preferred_element_type=jnp.float32,
    )


def columns_of(rows_ref, out_ref):
    for part in range(2):
        row = jnp.broadcast_to(rows_ref[part : part + 1, :OWN], (OWN, OWN))
        out_ref[part * OWN : (part + 1) * OWN] = jnp.transpose(row)


def split_columns(refs, out_ref):
    for part, ref in enumerate(refs):
        pieces = ref[:, 0:3].astype(jnp.float32)
        column = (pieces[:, 0:1] + pieces[:, 1:2]) + pieces[:, 2:3]
        out_ref[part * OWN : (part + 1) * OWN] = jnp.broadcast_to(column, (OWN, HD))


def rows_of(own_ref, other_ref, cols):
    return jnp.concatenate([own_ref[:, cols], other_ref[:, cols]], axis=0).astype(jnp.float32)


def row_block(array, part, width, column):
    row = part if array.shape[0] == REGION else 0
    return pl.BlockSpec((OWN, width), lambda j, *s: (row, column(j, *s)))


def whole(shape):
    return pl.BlockSpec(shape, lambda j, *s: (0, 0))


def forward_body(
    query_rows, heads, own_ref, other_ref, inverse_ref, gains_ref, slopes_ref, table_ref, keep_ref, *refs
):
    *out_refs, column_ref = refs
    step = pl.program_id(0)

    @pl.when(step == 0)
    def _():
        columns_of(inverse_ref, column_ref)

    inverse = column_ref[...]
    keep = keep_ref[:query_rows]
    ones = jnp.ones((REGION, HD), jnp.bfloat16)
    for head in range(heads):
        cols = pl.ds(head * HD, HD)
        gains = gains_ref[:, cols]
        hidden = rows_of(own_ref, other_ref, cols)
        normed_in = (hidden * inverse).astype(jnp.bfloat16).astype(jnp.float32)
        query = (normed_in[:query_rows] * gains[0:1]).astype(jnp.bfloat16)
        key = (normed_in * gains[1:2]).astype(jnp.bfloat16)
        value = (normed_in * gains[2:3]).astype(jnp.bfloat16)
        slope = slopes_ref[0, step * heads + head] * LOG2E
        scores = dot(query, key, 1, 1) * (SCALE * LOG2E) - slope * table_ref[:query_rows]
        exps = jnp.exp2(scores - jnp.max(scores, axis=1, keepdims=True)).astype(jnp.bfloat16)
        mixed = dot(exps, jnp.concatenate([value, ones], axis=1), 1, 0)
        attended = (mixed[:, :HD] / mixed[:, HD:]).astype(jnp.bfloat16).astype(jnp.float32)
        result = (hidden[:query_rows] + keep * attended).astype(jnp.bfloat16)
        out_refs[0][:, cols] = result[:OWN]
        if query_rows == REGION:
            out_refs[1][:, cols] = result


def forward(query_rows, own, other, inverse, gains, slopes, table, keep):
    width = STEP_HEADS * HD
    column = lambda j: j
    rows = [OWN] if query_rows == OWN else [OWN, REGION]
    return pl.pallas_call(
        functools.partial(forward_body, query_rows, STEP_HEADS),
        grid=(D // width,),
        in_specs=[
            row_block(own, 0, width, column),
            row_block(other, 1, width, column),
            whole((2, OWN)),
            pl.BlockSpec((3, width), lambda j: (0, j)),
            pl.BlockSpec(memory_space=pltpu.SMEM),
            whole((REGION, REGION)),
            whole((REGION, 1)),
        ],
        out_specs=[pl.BlockSpec((count, width), lambda j: (0, j)) for count in rows],
        out_shape=[jax.ShapeDtypeStruct((count, D), jnp.bfloat16) for count in rows],
        scratch_shapes=[pltpu.VMEM((REGION, HD), jnp.float32)],
        compiler_params=pltpu.CompilerParams(vmem_limit_bytes=VMEM_LIMIT),
        cost_estimate=FREE,
        name="attend" + str(query_rows),
    )(own, other, inverse, gains, slopes, table, keep)


def half_blocks(steps, width, *arrays):
    here = lambda j, s: j
    within = lambda j, s: s[0] * steps + j
    return [
        row_block(array, place % 2, width, within if array.shape[1] == D else here)
        for place, array in enumerate(arrays)
    ]


def tail_blocks():
    return [pl.BlockSpec((OWN, HD), lambda j, s: (0, HALF // HD))] * 2


def backward_body(
    heads,
    side_ref,
    own_ref,
    other_ref,
    cot_own_ref,
    cot_other_ref,
    inverse_own_ref,
    inverse_other_ref,
    gains_ref,
    slopes_ref,
    table_ref,
    keep_ref,
    grad_ref,
    small_ref,
    total_ref,
    column_ref,
):
    step = pl.program_id(0)
    first_head = side_ref[0] * (HEADS // 2) + step * heads
    keep = keep_ref[...]

    @pl.when(step == 0)
    def _():
        total_ref[...] = jnp.zeros_like(total_ref)
        small_ref[...] = jnp.zeros_like(small_ref)
        split_columns((inverse_own_ref, inverse_other_ref), column_ref)

    inverse = column_ref[...]

    for head in range(heads):
        cols = pl.ds(head * HD, HD)
        gains = gains_ref[:, cols]
        wide = rows_of(own_ref, other_ref, cols) * inverse
        normed_in = wide.astype(jnp.bfloat16).astype(jnp.float32)
        query = (normed_in * gains[0:1]).astype(jnp.bfloat16)
        key = (normed_in * gains[1:2]).astype(jnp.bfloat16)
        value = (normed_in * gains[2:3]).astype(jnp.bfloat16)
        masked = (rows_of(cot_own_ref, cot_other_ref, cols) * keep).astype(jnp.bfloat16)
        slope = slopes_ref[0, first_head + head] * LOG2E
        scores = dot(key, query, 1, 1) * (SCALE * LOG2E) - slope * table_ref[...]
        exps = jnp.exp2(scores - jnp.max(scores, axis=0, keepdims=True))
        probs = exps * (1.0 / jnp.sum(exps, axis=0, keepdims=True))
        grad_probs = dot(value, masked, 1, 1)
        inner = jnp.sum(probs * grad_probs, axis=0, keepdims=True)
        grad_scores = (probs * (grad_probs - inner) * SCALE).astype(jnp.bfloat16)
        grad_value = dot(probs.astype(jnp.bfloat16), masked, 1, 0)
        grad_key = dot(grad_scores, query, 1, 0)
        grad_query = dot(grad_scores, key, 0, 0)
        grad = grad_query * gains[0:1] + grad_key * gains[1:2] + grad_value * gains[2:3]
        grad_ref[:, cols] = grad.astype(jnp.bfloat16)
        total_ref[...] += grad * wide
        small_ref[0:1, pl.ds((step * heads + head) * HD, HD)] = jnp.sum(grad_query * normed_in, axis=0, keepdims=True)
        small_ref[1:2, pl.ds((step * heads + head) * HD, HD)] = jnp.sum(grad_key * normed_in, axis=0, keepdims=True)
        small_ref[2:3, pl.ds((step * heads + head) * HD, HD)] = jnp.sum(grad_value * normed_in, axis=0, keepdims=True)

    @pl.when(step == pl.num_programs(0) - 1)
    def _():
        moment = lax.dot_general(
            jnp.ones((8, HD), jnp.float32),
            total_ref[...],
            (((1,), (1,)), ((), ())),
            precision=lax.Precision.HIGHEST,
            preferred_element_type=jnp.float32,
        )
        small_ref[3:4, :REGION] = moment[0:1]


def backward(side, own, sent, other, cot_own, cot_other, gains, slopes, table, keep):
    width = STEP_HEADS * HD
    steps = HALF // width
    return pl.pallas_call(
        functools.partial(backward_body, STEP_HEADS),
        grid_spec=pltpu.PrefetchScalarGridSpec(
            num_scalar_prefetch=1,
            grid=(steps,),
            in_specs=[
                *half_blocks(steps, width, own, other, cot_own, cot_other),
                *tail_blocks(),
                pl.BlockSpec((3, width), lambda j, s: (0, s[0] * steps + j)),
                pl.BlockSpec(memory_space=pltpu.SMEM),
                whole((REGION, REGION)),
                whole((REGION, 1)),
            ],
            out_specs=[pl.BlockSpec((REGION, width), lambda j, s: (0, j)), whole((4, HALF))],
            scratch_shapes=[pltpu.VMEM((REGION, HD), jnp.float32)] * 2,
        ),
        out_shape=[
            jax.ShapeDtypeStruct((REGION, HALF), jnp.bfloat16),
            jax.ShapeDtypeStruct((4, HALF), jnp.float32),
        ],
        compiler_params=pltpu.CompilerParams(vmem_limit_bytes=VMEM_LIMIT),
        cost_estimate=FREE,
        name="differentiate",
    )(side, own, other, cot_own, cot_other, sent, other, gains, slopes, table, keep)


def combine_body(
    side_ref,
    own_ref,
    other_ref,
    cot_own_ref,
    cot_other_ref,
    grad_ref,
    inverse_own_ref,
    inverse_other_ref,
    small_ref,
    received_ref,
    out_ref,
    out_other,
    column_ref,
    mean_ref,
):
    @pl.when(pl.program_id(0) == 0)
    def _():
        split_columns((inverse_own_ref, inverse_other_ref), column_ref)
        for part in range(2):
            here, there = (pl.ds(part * OWN, OWN), pl.ds((1 - part) * OWN, OWN))
            total = small_ref[3:4, here] + received_ref[3:4, there]
            mean_ref[here] = jnp.transpose(jnp.broadcast_to(total, (OWN, OWN))) * (1.0 / D)

    for part, hidden, cot in ((0, own_ref, cot_own_ref), (1, other_ref, cot_other_ref)):
        rows = pl.ds(part * OWN, OWN)
        scale = column_ref[rows]
        mean = mean_ref[rows]
        for piece in range(out_ref.shape[1] // HD):
            cols = pl.ds(piece * HD, HD)
            wide = hidden[:, cols].astype(jnp.float32) * scale
            grad = (grad_ref[rows, cols].astype(jnp.float32) - wide * mean) * scale
            result = (cot[:, cols].astype(jnp.float32) + grad).astype(jnp.bfloat16)
            out_ref[rows, cols] = result
            if part == 1:
                out_other[:, cols] = result


def combine(side, own, sent, other, cot_own, cot_other, grad, small, received):
    width = STEP_HEADS * HD
    steps = HALF // width
    return pl.pallas_call(
        combine_body,
        grid_spec=pltpu.PrefetchScalarGridSpec(
            num_scalar_prefetch=1,
            grid=(steps,),
            in_specs=[
                *half_blocks(steps, width, own, other, cot_own, cot_other),
                pl.BlockSpec((REGION, width), lambda j, s: (0, j)),
                *tail_blocks(),
                whole((4, HALF)),
                whole((4, HALF)),
            ],
            out_specs=[
                pl.BlockSpec((count, width), lambda j, s: (0, j)) for count in (REGION, OWN)
            ],
            scratch_shapes=[pltpu.VMEM((REGION, HD), jnp.float32)] * 2,
        ),
        out_shape=[
            jax.ShapeDtypeStruct((count, HALF), jnp.bfloat16) for count in (REGION, OWN)
        ],
        compiler_params=pltpu.CompilerParams(vmem_limit_bytes=VMEM_LIMIT),
        cost_estimate=FREE,
        name="combine",
    )(side, own, other, cot_own, cot_other, grad, sent, other, small, received)


def after(value, *earlier):
    return lax.optimization_barrier((value, earlier))[0]


def with_inverse(half, inverse):
    first = lax.reduce_precision(inverse, 8, 7)
    second = lax.reduce_precision(inverse - first, 8, 7)
    pieces = jnp.stack([first, second, inverse - first - second], axis=1).astype(jnp.bfloat16)
    return jnp.concatenate([half, jnp.pad(pieces, ((0, 0), (0, HD - 3)))], axis=1)


def inverse_norm(hidden):
    wide = hidden.astype(jnp.float32)
    return lax.rsqrt(jnp.mean(wide * wide, axis=1) + 1e-05)


def on_device(
    acts_in, first_in, saved_one, cot_one, saved_two, cot_last, gains, slopes, ocean, places
):
    devices = lax.axis_size("seq")
    sections = lax.axis_size("section")
    my_index = lax.axis_index("seq")
    section_index = lax.axis_index("section")
    side = my_index % 2
    side_vec = side.astype(jnp.int32)[None]
    acts, saved_a, cot_a, saved_b = (acts_in[0], saved_one[0], cot_one[0], saved_two[0])
    gain_rows = gains[0]

    def flips(bits):
        return [(i, i ^ bits) for i in range(devices)]

    def swap(value):
        return lax.ppermute(value, "seq", flips(1))

    def swap_in(chosen, value):
        bases = [section * devices for section in chosen]
        pairs = [(base + i, base + (i ^ 1)) for base in bases for i in range(devices)]
        return lax.ppermute(value, ("section", "seq"), pairs)

    def shifted(value, steps):
        first, last = (max(0, -steps), min(sections, sections - steps))
        return lax.ppermute(value, "section", [(s, s + steps) for s in range(first, last)])

    def for_partner(matrix):
        return lax.dynamic_slice_in_dim(matrix, (1 - side) * HALF, HALF, 1)

    def for_me(matrix):
        return lax.dynamic_slice_in_dim(matrix, side * HALF, HALF, 1)

    def joined(mine, received):
        pair = jnp.concatenate([mine, received], axis=1)
        flipped = jnp.concatenate([received, mine], axis=1)
        return jnp.where(side == 0, pair, flipped)

    def region_order(vector):
        own = lax.dynamic_slice_in_dim(vector, my_index * OWN, OWN, vector.ndim - 1)
        start = (my_index + 1 - 2 * side) * OWN
        other = lax.dynamic_slice_in_dim(vector, start, OWN, vector.ndim - 1)
        return jnp.concatenate([own, other], axis=-1)

    place = region_order(places)
    wet = region_order(ocean)
    distance = (
        jnp.abs(place[0][:, None] - place[0][None, :])
        + jnp.abs(place[1][:, None] - place[1][None, :])
    ).astype(jnp.float32)
    by_query = jnp.where(wet[None, :] > 0, distance, FAR)
    by_key = jnp.where(wet[:, None] > 0, distance, FAR)
    keep = wet.astype(jnp.float32)[:, None]

    is_first = section_index == 0
    is_last = section_index == sections - 1

    with jax.named_scope("acts"):
        acts_other = swap(acts)
    saved_a_sent = with_inverse(for_partner(saved_a), inverse_norm(saved_a))
    saved_b_sent = with_inverse(for_partner(saved_b), inverse_norm(saved_b))
    with jax.named_scope("cot_a"):
        cot_a_other = swap(after(for_partner(cot_a), acts_other))
    with jax.named_scope("saved_a"):
        saved_a_other = swap(after(saved_a_sent, acts_other))
    inverse = jnp.stack([inverse_norm(acts), inverse_norm(acts_other)])
    out_one, out_region = forward(
        REGION, acts, acts_other, inverse, gain_rows, slopes, by_query, keep
    )
    with jax.named_scope("to_next"):
        from_before = shifted(out_region, 1)

    back = (side_vec, saved_a, saved_a_sent, after(saved_a_other, out_one), cot_a, cot_a_other)
    grad, small_a = backward(*back, gain_rows, slopes, by_key, keep)
    with jax.named_scope("small_a"):
        received_a = swap(small_a)
    with jax.named_scope("saved_b"):
        saved_b_other = swap(after(saved_b_sent, saved_a_other, out_one))
    with jax.named_scope("cot_last"):
        cot_last_send = after(for_partner(cot_last), saved_a_other, out_one)
        cot_last_other = swap_in((sections - 1,), cot_last_send)
    received_a = after(received_a, saved_b_other, cot_last_other)
    first, first_other = combine(*back, grad, small_a, received_a)
    with jax.named_scope("to_previous"):
        from_next = shifted(first, -1)
    with jax.named_scope("grad_one"):
        grad_one_part = swap(first_other)

    cot_b = jnp.concatenate([for_me(cot_last), cot_last_other], axis=0)
    cot_b = after(jnp.where(is_last, cot_b, from_next), from_before)
    with jax.named_scope("first_in"):
        first_in_other = swap_in((0,), after(first_in, from_next))
    back = (side_vec, saved_b, saved_b_sent, saved_b_other, cot_b, cot_b)
    grad, small_b = backward(*back, gain_rows, slopes, by_key, keep)
    small = small_b + jnp.where(jnp.arange(4)[:, None] < 3, small_a, 0.0)
    with jax.named_scope("small_b"):
        received_b = swap(small)
    received_b = after(received_b, grad_one_part, first_in_other)
    second, second_other = combine(*back, grad, small, received_b)
    with jax.named_scope("bwd_two"):
        bwd_two_part = swap(second_other)

    fed = jnp.concatenate([first_in, after(first_in_other, second_other)], axis=0)
    region_in = jnp.where(is_first, fed, from_before)
    inverse = inverse_norm(region_in).reshape(2, OWN)
    (fwd_two,) = forward(OWN, region_in, region_in, inverse, gain_rows, slopes, by_query, keep)

    gain_total = joined(small[:3], after(received_b, second_other)[:3])
    for bit in (4, 16):
        if bit < devices:
            with jax.named_scope("gain" + str(bit)):
                terms = [
                    lax.ppermute(gain_total, "seq", flips(bit * flip)) for flip in range(1, 4)
                ]
            gain_total = (gain_total + terms[0]) + (terms[1] + terms[2])
    if devices > 2:
        with jax.named_scope("gain2"):
            gain_total = gain_total + lax.ppermute(gain_total, "seq", flips(2))

    bwd_two_part = after(bwd_two_part, fwd_two, gain_total)

    grad_one = joined(first[:OWN], after(grad_one_part, second_other))
    bwd_two = joined(second[:OWN], bwd_two_part)
    return (out_one[None], grad_one[None], fwd_two[None], bwd_two[None], gain_total[None])


def solution(mesh):
    placed = (
        P("section", "seq", None),
        P("seq", None),
        P("section", "seq", None),
        P("section", "seq", None),
        P("section", "seq", None),
        P("seq", None),
        P("section", None, None),
        P("section", None),
        P(),
        P(),
    )
    return jax.shard_map(
        on_device,
        mesh=mesh,
        in_specs=placed,
        out_specs=(
            P("section", "seq", None),
            P("section", "seq", None),
            P("section", "seq", None),
            P("section", "seq", None),
            P("section", None, None),
        ),
        check_vma=False,
    )
```

```python
import functools

import jax
import jax.numpy as jnp
from jax import lax
from jax.experimental import pallas as pl
from jax.experimental.pallas import tpu as pltpu
from jax.sharding import PartitionSpec as P

D = 4096
HEADS = 32
HD = 128
REGION = 256
OWN = 128
HALF = D // 2
LATE = 3 * D // 4
LOG2E = 1.4426950408889634
SCALE = HD ** (-0.5)
FAR = 1e30
STEP_HEADS = 4
VMEM_LIMIT = 16 * 1024 * 1024
FREE = pl.CostEstimate(flops=0, bytes_accessed=0, transcendentals=0)


def dot(left, right, left_dim, right_dim):
    return lax.dot_general(
        left,
        right,
        (((left_dim,), (right_dim,)), ((), ())),
        preferred_element_type=jnp.float32,
    )


def columns_of(rows_ref, out_ref):
    for part in range(2):
        row = jnp.broadcast_to(rows_ref[part : part + 1, :OWN], (OWN, OWN))
        out_ref[part * OWN : (part + 1) * OWN] = jnp.transpose(row)


def split_columns(refs, out_ref):
    for part, ref in enumerate(refs):
        pieces = ref[:, 0:3].astype(jnp.float32)
        column = (pieces[:, 0:1] + pieces[:, 1:2]) + pieces[:, 2:3]
        out_ref[part * OWN : (part + 1) * OWN] = jnp.broadcast_to(column, (OWN, HD))


def rows_of(own_ref, other_ref, cols):
    return jnp.concatenate([own_ref[:, cols], other_ref[:, cols]], axis=0).astype(jnp.float32)


def row_block(array, part, width, column):
    row = part if array.shape[0] == REGION else 0
    return pl.BlockSpec((OWN, width), lambda j, *s: (row, column(j, *s)))


def whole(shape):
    return pl.BlockSpec(shape, lambda j, *s: (0, 0))


def forward_body(
    query_rows, heads, own_ref, other_ref, inverse_ref, gains_ref, slopes_ref, table_ref, keep_ref, *refs
):
    *out_refs, column_ref = refs
    step = pl.program_id(0)

    @pl.when(step == 0)
    def _():
        columns_of(inverse_ref, column_ref)

    inverse = column_ref[...]
    keep = keep_ref[:query_rows]
    ones = jnp.ones((REGION, HD), jnp.bfloat16)
    for head in range(heads):
        cols = pl.ds(head * HD, HD)
        gains = gains_ref[:, cols]
        hidden = rows_of(own_ref, other_ref, cols)
        normed_in = (hidden * inverse).astype(jnp.bfloat16).astype(jnp.float32)
        query = (normed_in[:query_rows] * gains[0:1]).astype(jnp.bfloat16)
        key = (normed_in * gains[1:2]).astype(jnp.bfloat16)
        value = (normed_in * gains[2:3]).astype(jnp.bfloat16)
        slope = slopes_ref[0, step * heads + head] * LOG2E
        scores = dot(query, key, 1, 1) * (SCALE * LOG2E) - slope * table_ref[:query_rows]
        exps = jnp.exp2(scores - jnp.max(scores, axis=1, keepdims=True)).astype(jnp.bfloat16)
        mixed = dot(exps, jnp.concatenate([value, ones], axis=1), 1, 0)
        attended = (mixed[:, :HD] / mixed[:, HD:]).astype(jnp.bfloat16).astype(jnp.float32)
        result = (hidden[:query_rows] + keep * attended).astype(jnp.bfloat16)
        out_refs[0][:, cols] = result[:OWN]
        if query_rows == REGION:
            out_refs[1][:, cols] = result


def forward(query_rows, own, other, inverse, gains, slopes, table, keep):
    width = STEP_HEADS * HD
    column = lambda j: j
    rows = [OWN] if query_rows == OWN else [OWN, REGION]
    return pl.pallas_call(
        functools.partial(forward_body, query_rows, STEP_HEADS),
        grid=(D // width,),
        in_specs=[
            row_block(own, 0, width, column),
            row_block(other, 1, width, column),
            whole((2, OWN)),
            pl.BlockSpec((3, width), lambda j: (0, j)),
            pl.BlockSpec(memory_space=pltpu.SMEM),
            whole((REGION, REGION)),
            whole((REGION, 1)),
        ],
        out_specs=[pl.BlockSpec((count, width), lambda j: (0, j)) for count in rows],
        out_shape=[jax.ShapeDtypeStruct((count, D), jnp.bfloat16) for count in rows],
        scratch_shapes=[pltpu.VMEM((REGION, HD), jnp.float32)],
        compiler_params=pltpu.CompilerParams(vmem_limit_bytes=VMEM_LIMIT),
        cost_estimate=FREE,
        name="attend" + str(query_rows),
    )(own, other, inverse, gains, slopes, table, keep)


def half_blocks(steps, width, *arrays):
    here = lambda j, s: j
    within = lambda j, s: s[0] * steps + j
    return [
        row_block(array, place % 2, width, within if array.shape[1] == D else here)
        for place, array in enumerate(arrays)
    ]


def tail_blocks():
    return [pl.BlockSpec((OWN, HD), lambda j, s: (0, HALF // HD))] * 2


def backward_body(
    heads,
    side_ref,
    own_ref,
    other_ref,
    cot_own_ref,
    cot_other_ref,
    inverse_own_ref,
    inverse_other_ref,
    gains_ref,
    slopes_ref,
    table_ref,
    keep_ref,
    grad_ref,
    small_ref,
    total_ref,
    column_ref,
):
    step = pl.program_id(0)
    first_head = side_ref[0] * (HEADS // 2) + step * heads
    keep = keep_ref[...]

    @pl.when(step == 0)
    def _():
        total_ref[...] = jnp.zeros_like(total_ref)
        small_ref[...] = jnp.zeros_like(small_ref)
        split_columns((inverse_own_ref, inverse_other_ref), column_ref)

    inverse = column_ref[...]

    for head in range(heads):
        cols = pl.ds(head * HD, HD)
        gains = gains_ref[:, cols]
        wide = rows_of(own_ref, other_ref, cols) * inverse
        normed_in = wide.astype(jnp.bfloat16).astype(jnp.float32)
        query = (normed_in * gains[0:1]).astype(jnp.bfloat16)
        key = (normed_in * gains[1:2]).astype(jnp.bfloat16)
        value = (normed_in * gains[2:3]).astype(jnp.bfloat16)
        masked = (rows_of(cot_own_ref, cot_other_ref, cols) * keep).astype(jnp.bfloat16)
        slope = slopes_ref[0, first_head + head] * LOG2E
        scores = dot(key, query, 1, 1) * (SCALE * LOG2E) - slope * table_ref[...]
        exps = jnp.exp2(scores - jnp.max(scores, axis=0, keepdims=True))
        probs = exps * (1.0 / jnp.sum(exps, axis=0, keepdims=True))
        grad_probs = dot(value, masked, 1, 1)
        inner = jnp.sum(probs * grad_probs, axis=0, keepdims=True)
        grad_scores = (probs * (grad_probs - inner) * SCALE).astype(jnp.bfloat16)
        grad_value = dot(probs.astype(jnp.bfloat16), masked, 1, 0)
        grad_key = dot(grad_scores, query, 1, 0)
        grad_query = dot(grad_scores, key, 0, 0)
        grad = grad_query * gains[0:1] + grad_key * gains[1:2] + grad_value * gains[2:3]
        grad_ref[:, cols] = grad.astype(jnp.bfloat16)
        total_ref[...] += grad * wide
        small_ref[0:1, pl.ds((step * heads + head) * HD, HD)] = jnp.sum(grad_query * normed_in, axis=0, keepdims=True)
        small_ref[1:2, pl.ds((step * heads + head) * HD, HD)] = jnp.sum(grad_key * normed_in, axis=0, keepdims=True)
        small_ref[2:3, pl.ds((step * heads + head) * HD, HD)] = jnp.sum(grad_value * normed_in, axis=0, keepdims=True)

    @pl.when(step == pl.num_programs(0) - 1)
    def _():
        moment = lax.dot_general(
            jnp.ones((8, HD), jnp.float32),
            total_ref[...],
            (((1,), (1,)), ((), ())),
            precision=lax.Precision.HIGHEST,
            preferred_element_type=jnp.float32,
        )
        small_ref[3:4, :REGION] = moment[0:1]


def backward(side, own, sent, other, cot_own, cot_other, gains, slopes, table, keep):
    width = STEP_HEADS * HD
    steps = HALF // width
    return pl.pallas_call(
        functools.partial(backward_body, STEP_HEADS),
        grid_spec=pltpu.PrefetchScalarGridSpec(
            num_scalar_prefetch=1,
            grid=(steps,),
            in_specs=[
                *half_blocks(steps, width, own, other, cot_own, cot_other),
                *tail_blocks(),
                pl.BlockSpec((3, width), lambda j, s: (0, s[0] * steps + j)),
                pl.BlockSpec(memory_space=pltpu.SMEM),
                whole((REGION, REGION)),
                whole((REGION, 1)),
            ],
            out_specs=[pl.BlockSpec((REGION, width), lambda j, s: (0, j)), whole((4, HALF))],
            scratch_shapes=[pltpu.VMEM((REGION, HD), jnp.float32)] * 2,
        ),
        out_shape=[
            jax.ShapeDtypeStruct((REGION, HALF), jnp.bfloat16),
            jax.ShapeDtypeStruct((4, HALF), jnp.float32),
        ],
        compiler_params=pltpu.CompilerParams(vmem_limit_bytes=VMEM_LIMIT),
        cost_estimate=FREE,
        name="differentiate",
    )(side, own, other, cot_own, cot_other, sent, other, gains, slopes, table, keep)


def combine_body(
    side_ref,
    own_ref,
    other_ref,
    cot_own_ref,
    cot_other_ref,
    grad_ref,
    inverse_own_ref,
    inverse_other_ref,
    small_ref,
    received_ref,
    out_ref,
    out_other,
    column_ref,
    mean_ref,
):
    @pl.when(pl.program_id(0) == 0)
    def _():
        split_columns((inverse_own_ref, inverse_other_ref), column_ref)
        for part in range(2):
            here, there = (pl.ds(part * OWN, OWN), pl.ds((1 - part) * OWN, OWN))
            total = small_ref[3:4, here] + received_ref[3:4, there]
            mean_ref[here] = jnp.transpose(jnp.broadcast_to(total, (OWN, OWN))) * (1.0 / D)

    for part, hidden, cot in ((0, own_ref, cot_own_ref), (1, other_ref, cot_other_ref)):
        rows = pl.ds(part * OWN, OWN)
        scale = column_ref[rows]
        mean = mean_ref[rows]
        for piece in range(out_ref.shape[1] // HD):
            cols = pl.ds(piece * HD, HD)
            wide = hidden[:, cols].astype(jnp.float32) * scale
            grad = (grad_ref[rows, cols].astype(jnp.float32) - wide * mean) * scale
            result = (cot[:, cols].astype(jnp.float32) + grad).astype(jnp.bfloat16)
            out_ref[rows, cols] = result
            if part == 1:
                out_other[:, cols] = result


def combine(side, own, sent, other, cot_own, cot_other, grad, small, received):
    width = STEP_HEADS * HD
    steps = HALF // width
    return pl.pallas_call(
        combine_body,
        grid_spec=pltpu.PrefetchScalarGridSpec(
            num_scalar_prefetch=1,
            grid=(steps,),
            in_specs=[
                *half_blocks(steps, width, own, other, cot_own, cot_other),
                pl.BlockSpec((REGION, width), lambda j, s: (0, j)),
                *tail_blocks(),
                whole((4, HALF)),
                whole((4, HALF)),
            ],
            out_specs=[
                pl.BlockSpec((count, width), lambda j, s: (0, j)) for count in (REGION, OWN)
            ],
            scratch_shapes=[pltpu.VMEM((REGION, HD), jnp.float32)] * 2,
        ),
        out_shape=[
            jax.ShapeDtypeStruct((count, HALF), jnp.bfloat16) for count in (REGION, OWN)
        ],
        compiler_params=pltpu.CompilerParams(vmem_limit_bytes=VMEM_LIMIT),
        cost_estimate=FREE,
        name="combine",
    )(side, own, other, cot_own, cot_other, grad, sent, other, small, received)


def after(value, *earlier):
    return lax.optimization_barrier((value, earlier))[0]


def with_inverse(half, inverse):
    first = lax.reduce_precision(inverse, 8, 7)
    second = lax.reduce_precision(inverse - first, 8, 7)
    pieces = jnp.stack([first, second, inverse - first - second], axis=1).astype(jnp.bfloat16)
    return jnp.concatenate([half, jnp.pad(pieces, ((0, 0), (0, HD - 3)))], axis=1)


def inverse_norm(hidden):
    wide = hidden.astype(jnp.float32)
    return lax.rsqrt(jnp.mean(wide * wide, axis=1) + 1e-05)


def on_device(
    acts_in, first_in, saved_one, cot_one, saved_two, cot_last, gains, slopes, ocean, places
):
    devices = lax.axis_size("seq")
    sections = lax.axis_size("section")
    my_index = lax.axis_index("seq")
    section_index = lax.axis_index("section")
    side = my_index % 2
    side_vec = side.astype(jnp.int32)[None]
    acts, saved_a, cot_a, saved_b = (acts_in[0], saved_one[0], cot_one[0], saved_two[0])
    gain_rows = gains[0]

    def flips(bits):
        return [(i, i ^ bits) for i in range(devices)]

    def swap(value):
        return lax.ppermute(value, "seq", flips(1))

    def swap_in(chosen, value):
        bases = [section * devices for section in chosen]
        pairs = [(base + i, base + (i ^ 1)) for base in bases for i in range(devices)]
        return lax.ppermute(value, ("section", "seq"), pairs)

    def shifted(value, steps):
        first, last = (max(0, -steps), min(sections, sections - steps))
        return lax.ppermute(value, "section", [(s, s + steps) for s in range(first, last)])

    def for_partner(matrix):
        return lax.dynamic_slice_in_dim(matrix, (1 - side) * HALF, HALF, 1)

    def for_me(matrix):
        return lax.dynamic_slice_in_dim(matrix, side * HALF, HALF, 1)

    def joined(mine, received):
        pair = jnp.concatenate([mine, received], axis=1)
        flipped = jnp.concatenate([received, mine], axis=1)
        return jnp.where(side == 0, pair, flipped)

    def region_order(vector):
        own = lax.dynamic_slice_in_dim(vector, my_index * OWN, OWN, vector.ndim - 1)
        start = (my_index + 1 - 2 * side) * OWN
        other = lax.dynamic_slice_in_dim(vector, start, OWN, vector.ndim - 1)
        return jnp.concatenate([own, other], axis=-1)

    place = region_order(places)
    wet = region_order(ocean)
    distance = (
        jnp.abs(place[0][:, None] - place[0][None, :])
        + jnp.abs(place[1][:, None] - place[1][None, :])
    ).astype(jnp.float32)
    by_query = jnp.where(wet[None, :] > 0, distance, FAR)
    by_key = jnp.where(wet[:, None] > 0, distance, FAR)
    keep = wet.astype(jnp.float32)[:, None]

    is_first = section_index == 0
    is_last = section_index == sections - 1

    with jax.named_scope("acts"):
        acts_other = swap(acts)
    saved_a_sent = with_inverse(for_partner(saved_a), inverse_norm(saved_a))
    saved_b_sent = with_inverse(for_partner(saved_b), inverse_norm(saved_b))
    with jax.named_scope("cot_a"):
        cot_a_other = swap(after(for_partner(cot_a), acts_other))
    with jax.named_scope("saved_a"):
        saved_a_other = swap(after(saved_a_sent, acts_other))
    inverse = jnp.stack([inverse_norm(acts), inverse_norm(acts_other)])
    out_one, out_region = forward(
        REGION, acts, acts_other, inverse, gain_rows, slopes, by_query, keep
    )
    with jax.named_scope("to_next"):
        from_before = shifted(out_region, 1)

    back = (side_vec, saved_a, saved_a_sent, after(saved_a_other, out_one), cot_a, cot_a_other)
    grad, small_a = backward(*back, gain_rows, slopes, by_key, keep)
    with jax.named_scope("small_a"):
        received_a = swap(small_a)
    with jax.named_scope("saved_b"):
        saved_b_other = swap(after(saved_b_sent, saved_a_other, out_one))
    with jax.named_scope("cot_last"):
        cot_last_send = after(for_partner(cot_last), saved_a_other, out_one)
        cot_last_other = swap_in((sections - 1,), cot_last_send)
    received_a = after(received_a, saved_b_other, cot_last_other)
    first, first_other = combine(*back, grad, small_a, received_a)
    with jax.named_scope("to_previous"):
        from_next = shifted(first, -1)
    with jax.named_scope("grad_one"):
        grad_one_part = swap(first_other)

    cot_b = jnp.concatenate([for_me(cot_last), cot_last_other], axis=0)
    cot_b = after(jnp.where(is_last, cot_b, from_next), from_before)
    with jax.named_scope("first_in"):
        first_in_other = swap_in((0,), after(first_in, from_next))
    back = (side_vec, saved_b, saved_b_sent, saved_b_other, cot_b, cot_b)
    grad, small_b = backward(*back, gain_rows, slopes, by_key, keep)
    small = small_b + jnp.where(jnp.arange(4)[:, None] < 3, small_a, 0.0)
    with jax.named_scope("small_b"):
        received_b = swap(small)
    received_b = after(received_b, grad_one_part, first_in_other)
    second, second_other = combine(*back, grad, small, received_b)
    with jax.named_scope("bwd_two"):
        bwd_two_part = swap(second_other)

    fed = jnp.concatenate([first_in, after(first_in_other, second_other)], axis=0)
    region_in = jnp.where(is_first, fed, from_before)
    inverse = inverse_norm(region_in).reshape(2, OWN)
    (fwd_two,) = forward(OWN, region_in, region_in, inverse, gain_rows, slopes, by_query, keep)

    gain_total = joined(small[:3], after(received_b, second_other)[:3])
    for flip_sets in ((4,), (8, 16, 24), (2, 32, 34)):
        if max(flip_sets) < devices:
            with jax.named_scope("gain" + str(flip_sets[0])):
                terms = [lax.ppermute(gain_total, "seq", flips(flip)) for flip in flip_sets]
            gain_total = gain_total + terms[0]
            if len(terms) > 1:
                gain_total = gain_total + (terms[1] + terms[2])

    bwd_two_part = after(bwd_two_part, fwd_two, gain_total)

    grad_one = joined(first[:OWN], after(grad_one_part, second_other))
    bwd_two = joined(second[:OWN], bwd_two_part)
    return (out_one[None], grad_one[None], fwd_two[None], bwd_two[None], gain_total[None])


def solution(mesh):
    placed = (
        P("section", "seq", None),
        P("seq", None),
        P("section", "seq", None),
        P("section", "seq", None),
        P("section", "seq", None),
        P("seq", None),
        P("section", None, None),
        P("section", None),
        P(),
        P(),
    )
    return jax.shard_map(
        on_device,
        mesh=mesh,
        in_specs=placed,
        out_specs=(
            P("section", "seq", None),
            P("section", "seq", None),
            P("section", "seq", None),
            P("section", "seq", None),
            P("section", None, None),
        ),
        check_vma=False,
    )
```
